32 devices in a mesh: cfg: 2 (over x), seq: 4 (over z), tp: 4 (over y, core).
Axes of the slice: x: 2, y: 2, z: 4, core: 2. Of those that a mesh axis runs over, the one named last changes fastest.
Arguments:
- image: bfloat16 [2048, 3072], P('seq', 'tp'), may hold values from -6 to 6
- text: bfloat16 [2, 1024, 3072], P('cfg', 'seq', 'tp'), may hold values from -6 to 6
- modulation: float32 [2, 2, 3, 3072], P('cfg'), may hold values from -3 to 3
- w_qkv: bfloat16 [3072, 4608], P('seq', 'tp'), may hold values from -0.109375 to 0.109375
- q_gain: float32 [128], replicated, may hold values from 0.5 to 12, as said below
- k_gain: float32 [128], replicated, may hold values from 0.5 to 12, as said below
- w_proj: bfloat16 [1536, 3072], P('tp', 'seq'), may hold values from -0.15625 to 0.15625
- text_len: int32 [2, 2], replicated, may hold values from 1 to 512
- text_tiles: int32 [2, 2, 4], replicated, may hold values from 0 to 3, each once within a row
- step_index: int32 [2], replicated, may hold values from 0 to 27
Outputs:
- guided: float32 [2048, 3072], P('seq', ('cfg', 'tp'))
- latent_next: float32 [2048, 3072], P('seq', ('cfg', 'tp'))
The draws below stay inside these ranges and needn't reach their ends.
Inputs may be any that keep to these rules, and one draw needn't show every extreme that they name: `q_gain`: each query and key norm gain is positive. `k_gain`: each query and key norm gain is positive. `text_tiles`: each row of four is an order of 0 to 3.
All inputs are finite; a program needn't handle non-finite values.
Results may differ from the reference program's by a relative error of at most 0.015.
The reference program's roundings to bfloat16 on the way count: a program that leaves them out, or rounds other values in their place, can miss the bound.
Values may be sent and summed in bfloat16 or wider, within the bound.
A program may use at most 128 MiB of HBM per device.

```python
import jax
import jax.numpy as jnp
from jax import lax

D = 3072
HEADS = 12
HD = 128
IMG = 1024
TXT = 512
STEPS = 28
PROMPTS = 2
IMGTOK = 2048
TXTTOK = 1024


def gain_draw(key):
    lower_end, upper_end = (0.5, 4.0)
    uniform_part = jax.random.uniform(key, (HD,), jnp.float32)
    return jnp.exp(jnp.log(lower_end) + uniform_part * (jnp.log(upper_end) - jnp.log(lower_end)))


def draw_q_gain(key, part):
    return gain_draw(jax.random.fold_in(key, 11))


def draw_k_gain(key, part):
    return gain_draw(jax.random.fold_in(key, 23))


def with_ends(array, rng, smallest, top_value):
    longest = array.shape.index(max(array.shape))
    spots = []
    for shift in (0, 1):
        where = [jax.random.randint(jax.random.fold_in(rng, axis), (), 0, length) for axis, length in enumerate(array.shape)]
        where[longest] = (where[longest] + shift) % array.shape[longest]
        spots.append(tuple(where))
    return array.at[spots[0]].set(smallest).at[spots[1]].set(top_value)


def block_levels(rng, shape, pieces, low, top_value):
    gain, own = 1.0, jax.random.fold_in(rng, 6)
    for dim, parts in pieces:
        steps = jnp.exp(jax.random.uniform(jax.random.fold_in(own, dim), (parts,), jnp.float32, low / len(pieces), top_value / len(pieces)))
        gain = gain * jnp.repeat(steps, shape[dim] // parts).reshape([-1 if axis == dim else 1 for axis in range(len(shape))])
    return gain


def gaussian(stream_key, shape, deviation, most, cuts=(), kind=jnp.bfloat16):
    entries = jax.random.normal(stream_key, shape, jnp.float32) * deviation
    if len(cuts) > 0:
        entries = block_levels(stream_key, shape, cuts, -0.22, 0.18) * entries
    return jnp.clip(entries, min=-most, max=most).astype(kind)


def setup_inputs(seed: int = 0) -> dict:
    key_of = jax.random.split(jax.random.key(seed), 11)
    return {
        "image": gaussian(key_of[0], (IMGTOK, D), 1.0, 6.0, ((0, 4), (1, 4))),
        "text": gaussian(key_of[1], (2, TXTTOK, D), 1.0, 6.0, ((0, 2), (1, 4), (2, 4))),
        "modulation": gaussian(key_of[2], (2, PROMPTS, 3, D), 0.5, 3.0, ((0, 2),), jnp.float32),
        "w_qkv": gaussian(key_of[3], (D, 3 * HEADS * HD), D ** -0.5, 0.109375, ((0, 4), (1, 4))),
        "q_gain": draw_q_gain(jax.random.fold_in(key_of[10], 71), 0),
        "k_gain": draw_k_gain(jax.random.fold_in(key_of[10], 71), 0),
        "w_proj": gaussian(key_of[6], (HEADS * HD, D), (HEADS * HD) ** -0.5, 0.15625, ((0, 4), (1, 4))),
        "text_len": with_ends(jax.random.randint(key_of[7], (2, PROMPTS), 1, TXT + 1), jax.random.fold_in(key_of[7], 1), 1, TXT).astype(jnp.int32),
        "text_tiles": jax.vmap(lambda own: jax.random.permutation(own, 4))(jax.random.split(key_of[8], 2 * PROMPTS)).reshape((2, PROMPTS, 4)).astype(jnp.int32),
        "step_index": jax.random.randint(key_of[9], (PROMPTS,), 0, STEPS).astype(jnp.int32),
    }


GUIDANCE = 4.0
SHIFT_FACTOR = 3.0
EPSILON = 1e-06

def layer_norm(rows):
    mean_value = lax.optimization_barrier(jnp.mean(rows, axis=-1, keepdims=True))
    centred = rows - mean_value
    spread = lax.optimization_barrier(jnp.mean(centred * centred, axis=-1, keepdims=True))
    return centred * lax.rsqrt(spread + EPSILON)

def head_norm(matrix, scaling):
    strength = lax.optimization_barrier(jnp.mean(matrix * matrix, axis=-1, keepdims=True))
    return (matrix * lax.rsqrt(strength + EPSILON) * scaling).astype(jnp.bfloat16)

def sigma_of(position):
    remaining = 1.0 - position / STEPS
    return SHIFT_FACTOR * remaining / (1.0 + (SHIFT_FACTOR - 1.0) * remaining)

def reference(image, text, modulation, w_qkv, q_gain, k_gain, w_proj, text_len, text_tiles, step_index):
    weight_four = w_qkv.reshape(D, HEADS, 3, HD)
    query_weight = weight_four[:, :, 0].reshape(D, HEADS * HD)
    pair_weight = weight_four[:, :, 1:].reshape(D, HEADS * 2 * HD)
    tile_rows = TXT // 4
    offsets = jnp.arange(tile_rows, dtype=jnp.int32)

    def velocity_of(half):

        def one_prompt(prompt):
            image_rows = lax.dynamic_slice_in_dim(image, prompt * IMG, IMG, 0)
            text_rows = lax.dynamic_slice_in_dim(text[half], prompt * TXT, TXT, 0)
            mods = lax.dynamic_index_in_dim(modulation[half], prompt, 0, keepdims=False)
            rows_all = jnp.concatenate([image_rows, text_rows], 0).astype(jnp.float32)
            normed = ((1.0 + mods[1]) * layer_norm(rows_all) + mods[0]).astype(jnp.bfloat16)
            query_sum = jnp.dot(normed[:IMG], query_weight, preferred_element_type=jnp.float32)
            pair_sum = jnp.dot(normed, pair_weight, preferred_element_type=jnp.float32)
            query = head_norm(query_sum.reshape(IMG, HEADS, HD), q_gain)
            pairs = pair_sum.reshape(IMG + TXT, HEADS, 2, HD)
            keys = head_norm(pairs[:, :, 0], k_gain)
            values = pairs[:, :, 1].astype(jnp.bfloat16)
            order_row = lax.dynamic_index_in_dim(text_tiles[half], prompt, 0, keepdims=False)
            length_now = lax.dynamic_index_in_dim(text_len[half], prompt, 0, keepdims=False)
            positions = (order_row[:, None] * tile_rows + offsets[None, :]).reshape(TXT)
            live_keys = jnp.concatenate([jnp.ones((IMG,), bool), positions < length_now])
            scores = jnp.einsum('qhd,khd->hqk', query.astype(jnp.float32), keys.astype(jnp.float32)) * HD ** (-0.5)
            scores = jnp.where(live_keys[None, None, :], scores, -jnp.inf)
            row_max = lax.optimization_barrier(jnp.max(scores, axis=-1, keepdims=True))
            exps = jnp.exp(scores - row_max)
            probs = (exps / lax.optimization_barrier(jnp.sum(exps, axis=-1, keepdims=True))).astype(jnp.bfloat16)
            attended = jnp.einsum('hqk,khd->qhd', probs.astype(jnp.float32), values.astype(jnp.float32))
            attended = attended.astype(jnp.bfloat16).reshape(IMG, HEADS * HD)
            projected = jnp.dot(attended, w_proj, preferred_element_type=jnp.float32)
            return (image_rows.astype(jnp.float32) + mods[2] * projected).astype(jnp.bfloat16)
        return lax.map(one_prompt, jnp.arange(PROMPTS, dtype=jnp.int32)).reshape(IMGTOK, D)
    cond_velocity = velocity_of(0).astype(jnp.float32)
    uncond_velocity = velocity_of(1).astype(jnp.float32)
    guided = uncond_velocity + GUIDANCE * (cond_velocity - uncond_velocity)
    step_now = step_index.astype(jnp.float32)
    step_size = sigma_of(step_now + 1.0) - sigma_of(step_now)
    latent_next = image.astype(jnp.float32) + jnp.repeat(step_size, IMG)[:, None] * guided
    return (guided, latent_next)
```

```python
import functools

import jax
import jax.numpy as jnp
from jax import lax
from jax.experimental import pallas as pl
from jax.experimental.pallas import tpu as pltpu
from jax.sharding import PartitionSpec as P

HD = 128
STEPS = 28


GUIDANCE = 4.0
SHIFT_FACTOR = 3.0
EPSILON = 1e-06


def from_partner(block, axis, stride):
    count = lax.axis_size(axis)
    route = []
    for low in range(count):
        high = low | 1 << stride
        if high != low and high < count:
            route += [(low, high), (high, low)]
    return lax.ppermute(block, axis, route)


def layer_norm(rows):
    mean_value = jnp.mean(rows, axis=-1, keepdims=True)
    centred = rows - mean_value
    spread = jnp.mean(centred * centred, axis=-1, keepdims=True)
    return centred * lax.rsqrt(spread + EPSILON)


def head_norm(matrix, scaling):
    strength = jnp.mean(matrix * matrix, axis=-1, keepdims=True)
    return (matrix * lax.rsqrt(strength + EPSILON) * scaling).astype(jnp.bfloat16)


def sigma_of(position):
    remaining = 1.0 - position / STEPS
    return SHIFT_FACTOR * remaining / (1.0 + (SHIFT_FACTOR - 1.0) * remaining)


MESH = pl.DeviceIdType.MESH


class Sender:
    def __init__(self):
        self.pending = []

    def push(self, src, dst, send, recv, to, when=None):
        copy = pltpu.make_async_remote_copy(
            src_ref=src, dst_ref=dst, send_sem=send, recv_sem=recv, device_id=to, device_id_type=MESH
        )
        guarded(when, copy.start)
        self.pending.append((when, copy.wait_send))

    def local(self, src, dst, sem, when=None):
        copy = pltpu.make_async_copy(src, dst, sem)
        guarded(when, copy.start)
        self.pending.append((when, copy.wait))

    def finish(self):
        for when, wait in self.pending:
            guarded(when, wait)


def guarded(when, act):
    if when is None:
        act()
    else:
        pl.when(when)(act)


def arrive(dst, sem, when=None):
    copy = pltpu.make_async_copy(dst, dst, sem)
    guarded(when, copy.wait)


def greet(partners):
    barrier = pltpu.get_barrier_semaphore()
    for device in partners:
        pl.semaphore_signal(barrier, inc=1, device_id=device, device_id_type=MESH)
    pl.semaphore_wait(barrier, len(partners))


def gather_kernel(
    n, tps, image, text, wqkv, wproj, acts, wfull, wcols, iblock,
    act_send, act_recv, fwd_send, z_send, z_recv, x_send, x_recv, k_send, k_recv, kx_send, kx_recv,
    own_send, own_recv, p_send, p_recv, i_send, i_recv,
):
    c, s, t = lax.axis_index("cfg"), lax.axis_index("seq"), lax.axis_index("tp")
    w, k, y = s % 2, t % 2, t // 2
    img, feats = image.shape
    txt = text.shape[1]
    depth, _ = wqkv.shape
    half = depth // 2
    chunk = half // 2 if (half // 2) % 16 == 0 else half
    chunks = half // chunk
    other_s = s + 1 - 2 * w
    other_k = t + 1 - 2 * k
    greet(
        [(c, (s + ds) % n, (t + dt) % tps) for ds in range(n) for dt in range(tps) if (ds, dt) != (0, 0)]
        + [(1 - c, s, t)]
    )
    out = Sender()
    is_main = k == w

    def rows_of(block, part, j):
        return pl.ds(pl.multiple_of(block * depth + part * half + j * chunk, 16), chunk)

    for d in range(1, n):
        to = (s + d) % n
        for j in range(chunks):
            out.push(
                wqkv.at[pl.ds(pl.multiple_of(c * half + j * chunk, 16), chunk)],
                wfull.at[rows_of(s, c, j)],
                z_send.at[d, j], z_recv.at[d, j], (c, to, t), when=(to % 2) == k,
            )
    def act_parts(block):
        cols = pl.ds(pl.multiple_of(block * feats, 128), feats)
        return [(0, acts.at[pl.ds(0, img), cols]), (1, acts.at[pl.ds(img, txt), cols])]

    sources = [image, text.at[0]]
    for part, dst in act_parts(t):
        out.push(sources[part], dst, act_send.at[tps // 2, part], act_recv.at[t, part], (c, other_s, 2 * y + w))
        for dy in range(1, tps // 2):
            to_y = (y + dy) % (tps // 2)
            out.push(sources[part], dst, act_send.at[dy, part], act_recv.at[t, part], (c, s, 2 * to_y + w))
        out.push(sources[part], dst, act_send.at[0, part], act_recv.at[t, part], (c, s, other_k), when=k != w)
        out.local(sources[part], dst, act_recv.at[t, part], when=k == w)
    own_rows = wfull.at[pl.ds(pl.multiple_of(s * depth, 16), depth)]
    out.local(wqkv, own_rows, own_recv, when=is_main)
    out.push(wqkv, own_rows, own_send, own_recv, (c, s, other_k), when=is_main)
    rows, width = wproj.shape
    pieces, _, piece = wcols.shape
    per = width // piece
    total_half = (n * width) // 2
    mine = (s * width) // total_half == c
    first = (s * width - c * total_half) // piece
    for h in range(per):
        index = jnp.maximum(first + h, 0)
        to_t = (index // pieces) % tps
        slot = index % pieces
        for ds in range(n):
            to_s = (s + ds) % n
            dst = wcols.at[slot, pl.ds(pl.multiple_of(t * rows, 16), rows)]
            src = wproj.at[:, pl.ds(h * piece, piece)] if per > 1 else wproj
            if ds == 0:
                same = to_t == t
                out.push(src, dst, p_send.at[ds, h], p_recv.at[slot, t], (c, to_s, to_t), when=mine & (to_t != t))
                out.local(src, dst, p_recv.at[slot, t], when=mine & same)
            else:
                out.push(src, dst, p_send.at[ds, h], p_recv.at[slot, t], (c, to_s, to_t), when=mine)
    block = iblock.shape[1]
    for h in range(2):
        index = 2 * t + h
        to_c, to_t = index // tps, index % tps
        src = image.at[:, pl.ds(h * block, block)]
        out.push(src, iblock, i_send.at[h], i_recv, (c, s, to_t), when=(to_c == c) & (to_t != t))
        out.local(src, iblock, i_recv, when=(to_c == c) & (to_t == t))

    far = k != w
    for dk in range(2):
        block_t = 2 * y + dk
        for part, dst in act_parts(block_t):
            arrive(dst, act_recv.at[block_t, part], when=far)
            for dy in range(1, tps // 2):
                to_y = (y + dy) % (tps // 2)
                out.push(
                    dst, dst, fwd_send.at[dk, dy, part], act_recv.at[block_t, part], (c, s, 2 * to_y + k), when=far
                )
    for d in range(1, n):
        origin = (s - d + n) % n
        for j in range(chunks):
            dst = wfull.at[rows_of(origin, c, j)]
            arrive(dst, z_recv.at[d, j], when=is_main)
            out.push(dst, dst, x_send.at[d, j], x_recv.at[d, j], (1 - c, s, t), when=is_main)
            out.push(dst, dst, k_send.at[d, j], k_recv.at[d, j], (c, s, other_k), when=is_main)
    for d in range(1, n):
        origin = (s - d + n) % n
        for j in range(chunks):
            dst = wfull.at[rows_of(origin, 1 - c, j)]
            arrive(dst, x_recv.at[d, j], when=is_main)
            out.push(dst, dst, kx_send.at[d, j], kx_recv.at[d, j], (c, s, other_k), when=is_main)
    for d in range(1, n):
        origin = (s - d + n) % n
        for j in range(chunks):
            arrive(wfull.at[rows_of(origin, c, j)], k_recv.at[d, j], when=~is_main)
            arrive(wfull.at[rows_of(origin, 1 - c, j)], kx_recv.at[d, j], when=~is_main)
    arrive(own_rows, own_recv, when=~is_main)
    for block_t in range(tps):
        for part, dst in act_parts(block_t):
            waited = far & (block_t // 2 == y)
            own = (k == w) & (block_t == t)
            arrive(dst, act_recv.at[block_t, part], when=~(waited | own))
    needed_first = t * pieces
    for slot in range(pieces):
        own_source = ((c * total_half + t * pieces * piece + slot * piece) // width) == s
        for from_t in range(tps):
            dst = wcols.at[slot, pl.ds(from_t * rows, rows)]
            arrive(dst, p_recv.at[slot, from_t], when=~(own_source & (from_t == t)))
    own_image = (c * tps + t) // 2 == t
    arrive(iblock, i_recv, when=~own_image)
    out.finish()


def gather_all(n, tps, image, text, wqkv, wproj):
    img, feats = image.shape
    txt = text.shape[1]
    depth, cols = wqkv.shape
    rows, width = wproj.shape
    block = feats // 2
    piece = min(width, block)
    pieces = block // piece
    half = depth // 2
    chunks = 2 if (half // 2) % 16 == 0 else 1
    per = width // piece
    dma = pltpu.SemaphoreType.DMA
    any_space = pl.BlockSpec(memory_space=pl.ANY)
    bf16 = jnp.bfloat16
    return pl.pallas_call(
        functools.partial(gather_kernel, n, tps),
        out_shape=(
            jax.ShapeDtypeStruct((img + txt, tps * feats), bf16),
            jax.ShapeDtypeStruct((n * depth, cols), bf16),
            jax.ShapeDtypeStruct((pieces, tps * rows, piece), bf16),
            jax.ShapeDtypeStruct((img, block), bf16),
        ),
        in_specs=[any_space] * 4,
        out_specs=(any_space,) * 4,
        scratch_shapes=[
            dma((tps // 2 + 1, 2)), dma((tps, 2)), dma((2, tps // 2, 2)),
            dma((n, chunks)), dma((n, chunks)), dma((n, chunks)), dma((n, chunks)),
            dma((n, chunks)), dma((n, chunks)), dma((n, chunks)), dma((n, chunks)),
            dma, dma, dma((n, per)), dma((pieces, tps)), dma((2,)), dma,
        ],
        compiler_params=pltpu.CompilerParams(collective_id=0, has_side_effects=True),
    )(image, text, wqkv, wproj)


def exchange_kernel(n, tps, attended, gathered, send, recv, fwd_send, fwd_recv):
    c, s, t = lax.axis_index("cfg"), lax.axis_index("seq"), lax.axis_index("tp")
    w, k, y = s % 2, t % 2, t // 2
    ys = tps // 2
    plane = s - w + k
    cols = attended.shape[1]
    other_k = t + 1 - 2 * k
    greet(
        [
            ((c + dc) % 2, s - w + (w + ds) % 2, (t + dt) % tps)
            for dc in range(2) for ds in range(2) for dt in range(tps) if (dc, ds, dt) != (0, 0, 0)
        ]
    )
    out = Sender()

    def place(half, head):
        return gathered.at[half, :, pl.ds(pl.multiple_of(head * cols, 128), cols)]

    for dc in (1, 0):
        for dy in reversed(range(ys)):
            to = ((c + dc) % 2, plane, 2 * ((y + dy) % ys) + w)
            dst = place(c, 2 * y + w)
            if dc == 0 and dy == 0:
                out.push(attended, dst, send.at[dc, dy], recv.at[dc, dy], to, when=k != w)
                out.local(attended, dst, recv.at[dc, dy], when=k == w)
            else:
                out.push(attended, dst, send.at[dc, dy], recv.at[dc, dy], to)
    for dc in range(2):
        for dy in range(ys):
            half, from_y = (c - dc + 2) % 2, (y - dy + ys) % ys
            dst = place(half, 2 * from_y + k)
            if dc == 0 and dy == 0:
                arrive(dst, recv.at[dc, dy], when=k != w)
                out.push(dst, dst, fwd_send.at[dc, dy], fwd_recv.at[dc, dy], (c, s, other_k), when=k != w)
                out.push(attended, dst, fwd_send.at[dc, dy], fwd_recv.at[dc, dy], (c, s, other_k), when=k == w)
            else:
                arrive(dst, recv.at[dc, dy])
                out.push(dst, dst, fwd_send.at[dc, dy], fwd_recv.at[dc, dy], (c, s, other_k))
    for dc in range(2):
        for dy in range(ys):
            half, from_y = (c - dc + 2) % 2, (y - dy + ys) % ys
            arrive(place(half, 2 * from_y + 1 - k), fwd_recv.at[dc, dy])
    out.finish()


def exchange(n, tps, attended):
    dma = pltpu.SemaphoreType.DMA
    any_space = pl.BlockSpec(memory_space=pl.ANY)
    rows, cols = attended.shape
    return pl.pallas_call(
        functools.partial(exchange_kernel, n, tps),
        out_shape=jax.ShapeDtypeStruct((2, rows, tps * cols), jnp.bfloat16),
        in_specs=[any_space],
        out_specs=any_space,
        scratch_shapes=[dma((2, tps // 2))] * 4,
        compiler_params=pltpu.CompilerParams(collective_id=1, has_side_effects=True),
    )(attended)


def local(image, text, modulation, w_qkv, q_gain, k_gain, w_proj, text_len, text_tiles, step_index):
    cfg_pos = lax.axis_index("cfg")
    seq_pos = lax.axis_index("seq")
    tp_pos = lax.axis_index("tp")
    tp_count = lax.axis_size("tp")
    seq_count = lax.axis_size("seq")
    prompt = seq_pos // 2
    part = tp_pos % 2
    mods = lax.dynamic_index_in_dim(modulation[0], prompt, 0, keepdims=False)
    block = image.shape[1] // 2
    width = image.shape[1] * tp_count
    gate_rows = mods[2].reshape(2 * tp_count, block)
    gate_own = lax.dynamic_index_in_dim(gate_rows, cfg_pos * tp_count + tp_pos, 0, keepdims=False)
    gate_sent = lax.dynamic_index_in_dim(gate_rows, (1 - cfg_pos) * tp_count + tp_pos, 0, keepdims=False)
    gate_far = from_partner(gate_sent, "cfg", 0)
    acts, piece, wcols, image_block = gather_all(seq_count, tp_count, image, text, w_qkv, w_proj)
    img_rows = image.shape[0]
    txt_rows = text.shape[1]
    normed = ((1.0 + mods[1]) * layer_norm(acts.astype(jnp.float32)) + mods[0]).astype(jnp.bfloat16)
    heads_dev = w_qkv.shape[1] // (3 * HD)
    count = piece.shape[0]
    blocks = piece.reshape(count, heads_dev, 3, HD)
    query_weight = blocks[:, :, 0].reshape(count, heads_dev * HD)
    pair_weight = blocks[:, :, 1:].reshape(count, heads_dev * 2 * HD)
    query_sum = jnp.dot(normed[:img_rows], query_weight, preferred_element_type=jnp.float32)
    pair_sum = jnp.dot(normed, pair_weight, preferred_element_type=jnp.float32)
    query = head_norm(query_sum.reshape(img_rows, heads_dev, HD), q_gain)
    pairs = pair_sum.reshape(-1, heads_dev, 2, HD)
    keys_own = head_norm(pairs[:, :, 0], k_gain)
    values_own = pairs[:, :, 1].astype(jnp.bfloat16)
    keys_far, values_far = from_partner((keys_own, values_own), "tp", 0)
    length_now = lax.dynamic_slice(text_len, (cfg_pos, prompt), (1, 1))[0, 0]
    order_row = lax.dynamic_slice(text_tiles, (cfg_pos, prompt, 0), (1, 1, 4))[0, 0]
    tile_rows = txt_rows // 2
    offsets = jnp.arange(tile_rows, dtype=jnp.int32)

    def text_live(slot_half):
        tile_ids = lax.dynamic_slice_in_dim(order_row, 2 * slot_half, 2, 0)
        positions = (tile_ids[:, None] * tile_rows + offsets[None, :]).reshape(txt_rows)
        return positions < length_now

    image_live = jnp.ones((img_rows,), bool)
    live_keys = jnp.concatenate([image_live, text_live(part), image_live, text_live(1 - part)])
    keys_all = jnp.concatenate([keys_own, keys_far], 0)
    values_all = jnp.concatenate([values_own, values_far], 0)
    scores = jnp.einsum(
        "qhd,khd->hqk", query, keys_all, preferred_element_type=jnp.float32
    ) * HD ** (-0.5)
    scores = jnp.where(live_keys[None, None, :], scores, -jnp.inf)
    row_max = jnp.max(scores, axis=-1, keepdims=True)
    exps = jnp.exp(scores - row_max)
    probs = (exps / jnp.sum(exps, axis=-1, keepdims=True)).astype(jnp.bfloat16)
    attended = jnp.einsum("hqk,khd->qhd", probs, values_all, preferred_element_type=jnp.float32)
    attended = attended.astype(jnp.bfloat16).reshape(img_rows, heads_dev * HD)
    gathered = exchange(seq_count, tp_count, attended)
    weight = wcols[0] if wcols.shape[0] == 1 else jnp.concatenate(list(wcols), axis=1)
    projected = jnp.dot(
        gathered.reshape(2 * img_rows, -1), weight, preferred_element_type=jnp.float32
    ).reshape(2, img_rows, block)
    own_image = image_block.astype(jnp.float32)
    gates = jnp.where(cfg_pos == 0, jnp.stack([gate_own, gate_far]), jnp.stack([gate_far, gate_own]))
    velocity = (own_image[None] + gates[:, None, :] * projected).astype(jnp.bfloat16)
    cond_velocity = velocity[0].astype(jnp.float32)
    uncond_velocity = velocity[1].astype(jnp.float32)
    guided = uncond_velocity + GUIDANCE * (cond_velocity - uncond_velocity)
    step_now = lax.dynamic_index_in_dim(step_index, prompt, 0, keepdims=False).astype(jnp.float32)
    step_size = sigma_of(step_now + 1.0) - sigma_of(step_now)
    latent_next = own_image + step_size * guided
    return (guided, latent_next)


def solution(mesh):
    in_specs = (
        P("seq", "tp"),
        P("cfg", "seq", "tp"),
        P("cfg", None, None, None),
        P("seq", "tp"),
        P(),
        P(),
        P("tp", "seq"),
        P(),
        P(),
        P(),
    )
    out_specs = (P("seq", ("cfg", "tp")), P("seq", ("cfg", "tp")))
    return jax.shard_map(local, mesh=mesh, in_specs=in_specs, out_specs=out_specs, check_vma=False)
```

```python
import functools

import jax
import jax.numpy as jnp
from jax import lax
from jax.experimental import pallas as pl
from jax.experimental.pallas import tpu as pltpu
from jax.sharding import PartitionSpec as P

HD = 128
STEPS = 28


GUIDANCE = 4.0
SHIFT_FACTOR = 3.0
EPSILON = 1e-06


def from_partner(block, axis, stride):
    count = lax.axis_size(axis)
    route = []
    for low in range(count):
        high = low | 1 << stride
        if high != low and high < count:
            route += [(low, high), (high, low)]
    return lax.ppermute(block, axis, route)


def layer_norm(rows):
    mean_value = jnp.mean(rows, axis=-1, keepdims=True)
    centred = rows - mean_value
    spread = jnp.mean(centred * centred, axis=-1, keepdims=True)
    return centred * lax.rsqrt(spread + EPSILON)


def head_norm(matrix, scaling):
    strength = jnp.mean(matrix * matrix, axis=-1, keepdims=True)
    return (matrix * lax.rsqrt(strength + EPSILON) * scaling).astype(jnp.bfloat16)


def sigma_of(position):
    remaining = 1.0 - position / STEPS
    return SHIFT_FACTOR * remaining / (1.0 + (SHIFT_FACTOR - 1.0) * remaining)


MESH = pl.DeviceIdType.MESH
TEXT = 2


class Sender:
    def __init__(self):
        self.pending = []

    def push(self, src, dst, send, recv, to, when=None):
        copy = pltpu.make_async_remote_copy(
            src_ref=src, dst_ref=dst, send_sem=send, recv_sem=recv, device_id=to, device_id_type=MESH
        )
        guarded(when, copy.start)
        self.pending.append((when, copy.wait_send))

    def local(self, src, dst, sem, when=None):
        copy = pltpu.make_async_copy(src, dst, sem)
        guarded(when, copy.start)
        self.pending.append((when, copy.wait))

    def finish(self):
        for when, wait in self.pending:
            guarded(when, wait)


def guarded(when, act):
    if when is None:
        act()
    else:
        pl.when(when)(act)


def arrive(dst, sem, when=None):
    copy = pltpu.make_async_copy(dst, dst, sem)
    guarded(when, copy.wait)


def greet(partners):
    barrier = pltpu.get_barrier_semaphore()
    for device in partners:
        pl.semaphore_signal(barrier, inc=1, device_id=device, device_id_type=MESH)
    pl.semaphore_wait(barrier, len(partners))


def gather_kernel(
    n, tps, image, text, wqkv, wproj, mods, gains, queries, keys, values, wcols, iblock,
    acts, wfull, normed, total, stage, act_send, act_recv, near_send, ix_send, fwd_send, z_send, z_recv, x_send, x_recv, k_send, k_recv, kx_send, kx_recv,
    own_send, own_recv, st_send, st_recv, p_send, p_recv, i_send, i_recv,
):
    c, s, t = lax.axis_index("cfg"), lax.axis_index("seq"), lax.axis_index("tp")
    w, k, y = s % 2, t % 2, t // 2
    img, feats = image.shape
    txt = text.shape[1]
    depth, _ = wqkv.shape
    half = depth // 2
    chunk = half // 2 if (half // 2) % 16 == 0 else half
    chunks = half // chunk
    other_s = s + 1 - 2 * w
    other_k = t + 1 - 2 * k
    greet(
        [(c, (s + ds) % n, (t + dt) % tps) for ds in range(n) for dt in range(tps) if (ds, dt) != (0, 0)]
        + [(1 - c, s, t)]
    )
    out = Sender()
    is_main = k == w

    hrows = img // 2
    ys = tps // 2

    def act_part(block, part):
        cols = pl.ds(pl.multiple_of(block * feats, 128), feats)
        if part is TEXT:
            return acts.at[pl.ds(img, txt), cols]
        return acts.at[pl.ds(pl.multiple_of(part * hrows, 16), hrows), cols]

    def act_source(part):
        return text.at[0] if part is TEXT else image.at[pl.ds(pl.multiple_of(part * hrows, 16), hrows)]

    for part in (TEXT, c):
        dst = act_part(t, part)
        index = 1 if part is TEXT else 0
        src = act_source(part)
        out.push(src, dst, act_send.at[ys, index], act_recv.at[t, part], (c, other_s, 2 * y + w))
        for dy in range(1, ys):
            to_y = (y + dy) % ys
            out.push(src, dst, act_send.at[dy, index], act_recv.at[t, part], (c, s, 2 * to_y + w))
    for part in (0, 1, TEXT):
        src, dst = act_source(part), act_part(t, part)
        out.push(src, dst, near_send.at[part], act_recv.at[t, part], (c, s, other_k), when=k != w)
        guarded(k == w, pltpu.make_async_copy(src, dst, act_recv.at[t, part]).start)
    def rows_of(block, part, j):
        return pl.ds(pl.multiple_of(block * depth + part * half + j * chunk, 16), chunk)

    for d in range(1, n):
        to = (s + d) % n
        for j in range(chunks):
            out.push(
                wqkv.at[pl.ds(pl.multiple_of(c * half + j * chunk, 16), chunk)],
                wfull.at[rows_of(s, c, j)],
                z_send.at[d, j], z_recv.at[d, j], (c, to, t), when=(to % 2) == k,
            )
    own_rows = wfull.at[pl.ds(pl.multiple_of(s * depth, 16), depth)]
    own_copy = pltpu.make_async_copy(wqkv, own_rows, own_recv)
    guarded(is_main, own_copy.start)
    out.push(wqkv, own_rows, own_send, own_recv, (c, s, other_k), when=is_main)
    rows, width = wproj.shape
    pieces, _, piece = wcols.shape
    per = width // piece
    groups = n // 2
    mine = s // groups == c
    spot = s % groups
    guarded(mine, pltpu.make_async_copy(wproj, stage.at[spot], st_recv.at[0]).start)
    for ds in range(1, n):
        out.push(wproj, stage.at[spot], st_send.at[ds], st_recv.at[ds], (c, (s + ds) % n, t), when=mine)
    block = iblock.shape[1]
    for h in range(2):
        index = 2 * t + h
        to_c, to_t = index // tps, index % tps
        src = image.at[:, pl.ds(h * block, block)]
        out.push(src, iblock, i_send.at[h], i_recv, (c, s, to_t), when=(to_c == c) & (to_t != t))
        out.local(src, iblock, i_recv, when=(to_c == c) & (to_t == t))

    far = k != w
    for dk in range(2):
        block_t = 2 * y + dk
        for part in (TEXT, c):
            index = 1 if part is TEXT else 0
            dst = act_part(block_t, part)
            arrive(dst, act_recv.at[block_t, part], when=far)
            for dy in range(1, ys):
                to_y = (y + dy) % ys
                out.push(
                    dst, dst, fwd_send.at[dk, dy, index], act_recv.at[block_t, part], (c, s, 2 * to_y + k), when=far
                )
            if part is not TEXT:
                out.push(dst, dst, ix_send.at[dk], act_recv.at[block_t, part], (1 - c, s, t), when=far)

    def swap_images():
        for dy in range(1, ys):
            for dk in range(2):
                block_t = 2 * ((y + dy) % ys) + dk
                dst = act_part(block_t, c)
                arrive(dst, act_recv.at[block_t, c])
                out.push(dst, dst, ix_send.at[2 * dy + dk], act_recv.at[block_t, c], (1 - c, s, t))

    for d in range(1, n):
        origin = (s - d + n) % n
        for j in range(chunks):
            dst = wfull.at[rows_of(origin, c, j)]
            arrive(dst, z_recv.at[d, j], when=is_main)
            out.push(dst, dst, x_send.at[d, j], x_recv.at[d, j], (1 - c, s, t), when=is_main)
            out.push(dst, dst, k_send.at[d, j], k_recv.at[d, j], (c, s, other_k), when=is_main)
        if d == 1:
            swap_images()
    for block_t in range(tps):
        here = block_t // 2 == y
        for part in (0, 1, TEXT):
            done = (here & far & ((part is TEXT) | (c == part))) | (~here & (c == part))
            arrive(act_part(block_t, part), act_recv.at[block_t, part], when=~done)
    fan = 32

    @pl.loop(0, (img + txt) // fan)
    def _(step):
        at = pl.ds(pl.multiple_of(step * fan, fan), fan)
        rows_in = acts[at].astype(jnp.float32)
        normed[at] = ((1.0 + mods[1:2]) * layer_norm(rows_in) + mods[0:1]).astype(jnp.bfloat16)

    wide = wfull.shape[1] // 3
    band = (img + txt) // 3

    def multiply(start, size, fresh):
        at_k = pl.ds(pl.multiple_of(start, 128), size)

        @pl.loop(0, 3)
        def _(step):
            at = pl.ds(pl.multiple_of(step * band, 16), band)
            for third in range(3):
                at_c = pl.ds(third * wide, wide)
                product = jnp.dot(normed[at, at_k], wfull[at_k, at_c], preferred_element_type=jnp.float32)
                total[at, at_c] = product if fresh else total[at, at_c] + product

    by_block = depth % 128 == 0
    arrive(own_rows, own_recv, when=~is_main)
    guarded(is_main, own_copy.wait)
    if by_block:
        multiply(s * depth, depth, True)
    for group in range(groups):
        origin = c * groups + group
        for ds in range(n):
            arrive(stage.at[group], st_recv.at[ds], when=(s - origin + n) % n == ds)
        for h in range(per):
            to_t = (group * per + h) // pieces
            slot = (group * per + h) % pieces
            src = stage.at[group, :, pl.ds(h * piece, piece)] if per > 1 else stage.at[group]
            dst = wcols.at[slot, pl.ds(pl.multiple_of(t * rows, 16), rows)]
            out.push(src, dst, p_send.at[group, h], p_recv.at[slot, t], (c, s, to_t), when=to_t != t)
            out.local(src, dst, p_recv.at[slot, t], when=to_t == t)
    for d in range(1, n):
        origin = (s - d + n) % n
        for j in range(chunks):
            dst = wfull.at[rows_of(origin, 1 - c, j)]
            arrive(dst, x_recv.at[d, j], when=is_main)
            out.push(dst, dst, kx_send.at[d, j], kx_recv.at[d, j], (c, s, other_k), when=is_main)
        for j in range(chunks):
            arrive(wfull.at[rows_of(origin, c, j)], k_recv.at[d, j], when=~is_main)
            arrive(wfull.at[rows_of(origin, 1 - c, j)], kx_recv.at[d, j], when=~is_main)
        if by_block:
            multiply(origin * depth, depth, False)
    if not by_block:
        multiply(0, n * depth, True)
    for head in range(wfull.shape[1] // (3 * HD)):
        at_h = pl.ds(head * HD, HD)
        queries[:, at_h] = head_norm(total[pl.ds(0, img), pl.ds(head * 3 * HD, HD)], gains[0:1])
        keys[:, at_h] = head_norm(total[:, pl.ds(head * 3 * HD + HD, HD)], gains[1:2])
        values[:, at_h] = total[:, pl.ds(head * 3 * HD + 2 * HD, HD)].astype(jnp.bfloat16)
    for slot in range(pieces):
        for from_t in range(tps):
            arrive(wcols.at[slot, pl.ds(from_t * rows, rows)], p_recv.at[slot, from_t], when=t != from_t)
    own_image = (c * tps + t) // 2 == t
    arrive(iblock, i_recv, when=~own_image)
    out.finish()


def gather_all(n, tps, image, text, wqkv, wproj, mods, gains):
    img, feats = image.shape
    txt = text.shape[1]
    depth, cols = wqkv.shape
    rows, width = wproj.shape
    block = feats // 2
    piece = min(width, block)
    pieces = block // piece
    half = depth // 2
    chunks = 2 if (half // 2) % 16 == 0 else 1
    per = width // piece
    dma = pltpu.SemaphoreType.DMA
    any_space = pl.BlockSpec(memory_space=pl.ANY)
    vmem = pl.BlockSpec(memory_space=pltpu.VMEM)
    bf16 = jnp.bfloat16
    return pl.pallas_call(
        functools.partial(gather_kernel, n, tps),
        out_shape=(
            jax.ShapeDtypeStruct((img, cols // 3), bf16),
            jax.ShapeDtypeStruct((img + txt, cols // 3), bf16),
            jax.ShapeDtypeStruct((img + txt, cols // 3), bf16),
            jax.ShapeDtypeStruct((pieces, tps * rows, piece), bf16),
            jax.ShapeDtypeStruct((img, block), bf16),
        ),
        in_specs=[any_space] * 4 + [vmem] * 2,
        out_specs=(vmem,) * 3 + (any_space,) * 2,
        scratch_shapes=[
            pltpu.VMEM((img + txt, tps * feats), bf16),
            pltpu.VMEM((n * depth, cols), bf16),
            pltpu.VMEM((img + txt, tps * feats), bf16),
            pltpu.VMEM((img + txt, cols), jnp.float32),
            pltpu.VMEM((n // 2, rows, width), bf16),
            dma((tps // 2 + 1, 2)), dma((tps, 3)), dma((3,)), dma((tps,)), dma((2, tps // 2, 2)),
            dma((n, chunks)), dma((n, chunks)), dma((n, chunks)), dma((n, chunks)),
            dma((n, chunks)), dma((n, chunks)), dma((n, chunks)), dma((n, chunks)),
            dma, dma, dma((n,)), dma((n,)), dma((n // 2, per)), dma((pieces, tps)), dma((2,)), dma,
        ],
        compiler_params=pltpu.CompilerParams(collective_id=0, has_side_effects=True, vmem_limit_bytes=48 * 1024 * 1024),
    )(image, text, wqkv, wproj, mods, gains)


def exchange_kernel(n, tps, attended, gathered, send, recv, fwd_send, fwd_recv):
    c, s, t = lax.axis_index("cfg"), lax.axis_index("seq"), lax.axis_index("tp")
    w, k, y = s % 2, t % 2, t // 2
    ys = tps // 2
    plane = s - w + k
    cols = attended.shape[1]
    other_k = t + 1 - 2 * k
    greet(
        [
            ((c + dc) % 2, s - w + (w + ds) % 2, (t + dt) % tps)
            for dc in range(2) for ds in range(2) for dt in range(tps) if (dc, ds, dt) != (0, 0, 0)
        ]
    )
    out = Sender()

    def place(half, head):
        return gathered.at[half, :, pl.ds(pl.multiple_of(head * cols, 128), cols)]

    for dc in (1, 0):
        for dy in reversed(range(ys)):
            to = ((c + dc) % 2, plane, 2 * ((y + dy) % ys) + w)
            dst = place(c, 2 * y + w)
            if dc == 0 and dy == 0:
                out.push(attended, dst, send.at[dc, dy], recv.at[dc, dy], to, when=k != w)
                out.local(attended, dst, recv.at[dc, dy], when=k == w)
            else:
                out.push(attended, dst, send.at[dc, dy], recv.at[dc, dy], to)
    for dc in range(2):
        for dy in range(ys):
            half, from_y = (c - dc + 2) % 2, (y - dy + ys) % ys
            dst = place(half, 2 * from_y + k)
            if dc == 0 and dy == 0:
                arrive(dst, recv.at[dc, dy], when=k != w)
                out.push(dst, dst, fwd_send.at[dc, dy], fwd_recv.at[dc, dy], (c, s, other_k), when=k != w)
                out.push(attended, dst, fwd_send.at[dc, dy], fwd_recv.at[dc, dy], (c, s, other_k), when=k == w)
            else:
                arrive(dst, recv.at[dc, dy])
                out.push(dst, dst, fwd_send.at[dc, dy], fwd_recv.at[dc, dy], (c, s, other_k))
    for dc in range(2):
        for dy in range(ys):
            half, from_y = (c - dc + 2) % 2, (y - dy + ys) % ys
            arrive(place(half, 2 * from_y + 1 - k), fwd_recv.at[dc, dy])
    out.finish()


def exchange(n, tps, attended):
    dma = pltpu.SemaphoreType.DMA
    any_space = pl.BlockSpec(memory_space=pl.ANY)
    rows, cols = attended.shape
    return pl.pallas_call(
        functools.partial(exchange_kernel, n, tps),
        out_shape=jax.ShapeDtypeStruct((2, rows, tps * cols), jnp.bfloat16),
        in_specs=[any_space],
        out_specs=any_space,
        scratch_shapes=[dma((2, tps // 2))] * 4,
        compiler_params=pltpu.CompilerParams(collective_id=1, has_side_effects=True),
    )(attended)


def local(image, text, modulation, w_qkv, q_gain, k_gain, w_proj, text_len, text_tiles, step_index):
    cfg_pos = lax.axis_index("cfg")
    seq_pos = lax.axis_index("seq")
    tp_pos = lax.axis_index("tp")
    tp_count = lax.axis_size("tp")
    seq_count = lax.axis_size("seq")
    prompt = seq_pos // 2
    part = tp_pos % 2
    mods = lax.dynamic_index_in_dim(modulation[0], prompt, 0, keepdims=False)
    block = image.shape[1] // 2
    width = image.shape[1] * tp_count
    gate_rows = mods[2].reshape(2 * tp_count, block)
    gate_own = lax.dynamic_index_in_dim(gate_rows, cfg_pos * tp_count + tp_pos, 0, keepdims=False)
    gate_sent = lax.dynamic_index_in_dim(gate_rows, (1 - cfg_pos) * tp_count + tp_pos, 0, keepdims=False)
    gate_far = from_partner(gate_sent, "cfg", 0)
    query, keys_own, values_own, wcols, image_block = gather_all(
        seq_count, tp_count, image, text, w_qkv, w_proj, mods[:2], jnp.stack([q_gain, k_gain])
    )
    img_rows = image.shape[0]
    txt_rows = text.shape[1]
    heads_dev = w_qkv.shape[1] // (3 * HD)
    query = query.reshape(img_rows, heads_dev, HD)
    keys_own = keys_own.reshape(-1, heads_dev, HD)
    values_own = values_own.reshape(-1, heads_dev, HD)
    keys_far, values_far = from_partner((keys_own, values_own), "tp", 0)
    length_now = lax.dynamic_slice(text_len, (cfg_pos, prompt), (1, 1))[0, 0]
    order_row = lax.dynamic_slice(text_tiles, (cfg_pos, prompt, 0), (1, 1, 4))[0, 0]
    tile_rows = txt_rows // 2
    offsets = jnp.arange(tile_rows, dtype=jnp.int32)

    def text_live(slot_half):
        tile_ids = lax.dynamic_slice_in_dim(order_row, 2 * slot_half, 2, 0)
        positions = (tile_ids[:, None] * tile_rows + offsets[None, :]).reshape(txt_rows)
        return positions < length_now

    image_live = jnp.ones((img_rows,), bool)
    live_keys = jnp.concatenate([image_live, text_live(part), image_live, text_live(1 - part)])
    keys_all = jnp.concatenate([keys_own, keys_far], 0)
    values_all = jnp.concatenate([values_own, values_far], 0)
    scores = jnp.einsum(
        "qhd,khd->hqk", query, keys_all, preferred_element_type=jnp.float32
    ) * HD ** (-0.5)
    scores = jnp.where(live_keys[None, None, :], scores, -jnp.inf)
    row_max = jnp.max(scores, axis=-1, keepdims=True)
    exps = jnp.exp(scores - row_max)
    probs = (exps / jnp.sum(exps, axis=-1, keepdims=True)).astype(jnp.bfloat16)
    attended = jnp.einsum("hqk,khd->qhd", probs, values_all, preferred_element_type=jnp.float32)
    attended = attended.astype(jnp.bfloat16).reshape(img_rows, heads_dev * HD)
    gathered = exchange(seq_count, tp_count, attended)
    weight = wcols[0] if wcols.shape[0] == 1 else jnp.concatenate(list(wcols), axis=1)
    projected = jnp.dot(
        gathered.reshape(2 * img_rows, -1), weight, preferred_element_type=jnp.float32
    ).reshape(2, img_rows, block)
    own_image = image_block.astype(jnp.float32)
    gates = jnp.where(cfg_pos == 0, jnp.stack([gate_own, gate_far]), jnp.stack([gate_far, gate_own]))
    velocity = (own_image[None] + gates[:, None, :] * projected).astype(jnp.bfloat16)
    cond_velocity = velocity[0].astype(jnp.float32)
    uncond_velocity = velocity[1].astype(jnp.float32)
    guided = uncond_velocity + GUIDANCE * (cond_velocity - uncond_velocity)
    step_now = lax.dynamic_index_in_dim(step_index, prompt, 0, keepdims=False).astype(jnp.float32)
    step_size = sigma_of(step_now + 1.0) - sigma_of(step_now)
    latent_next = own_image + step_size * guided
    return (guided, latent_next)


def solution(mesh):
    in_specs = (
        P("seq", "tp"),
        P("cfg", "seq", "tp"),
        P("cfg", None, None, None),
        P("seq", "tp"),
        P(),
        P(),
        P("tp", "seq"),
        P(),
        P(),
        P(),
    )
    out_specs = (P("seq", ("cfg", "tp")), P("seq", ("cfg", "tp")))
    return jax.shard_map(local, mesh=mesh, in_specs=in_specs, out_specs=out_specs, check_vma=False)
```
